32 devices in a mesh: dp: 16 (over z, y, core), tensor: 2 (over x).
Axes of the slice: x: 2, y: 2, z: 4, core: 2. Of those that a mesh axis runs over, the one named last changes fastest.
Arguments:
- output_gradient: bfloat16 [6144, 8192], P(('dp', 'tensor')), may hold values from -6 to 6
- attention_input: bfloat16 [6144, 8192], P('dp', 'tensor'), may hold values from -6 to 6
- projection_weight: bfloat16 [8192, 8192], P('tensor', 'dp'), may hold values from -0.0625 to 0.0625
- adapter_down: float32 [16, 8192, 64], P('dp', 'tensor'), may hold values from -0.0625 to 0.0625
- adapter_up: float32 [16, 64, 8192], P('dp', None, 'tensor'), may hold values from -0.0625 to 0.0625
- down_first_moment: float32 [16, 8192, 64], P('dp', 'tensor'), may hold values from -0.75 to 0.75
- down_second_moment: float32 [16, 8192, 64], P('dp', 'tensor'), may hold values from 0.001 to 0.01
- up_first_moment: float32 [16, 64, 8192], P('dp', None, 'tensor'), may hold values from -0.75 to 0.75
- up_second_moment: float32 [16, 64, 8192], P('dp', None, 'tensor'), may hold values from 0.001 to 0.01
- tenant_lookup: int32 [16], replicated, may hold values from 0 to 3, never falling along the last dimension, each value on 1 to 13 neighbouring positions
- active_token_rows: int32 [16], P('dp'), may hold values from 128 to 384, as said below
Outputs:
- input_gradient: bfloat16 [6144, 8192], P('dp', 'tensor')
- fresh_adapter_down: float32 [16, 8192, 64], P('dp', 'tensor')
- fresh_down_first_moment: float32 [16, 8192, 64], P('dp', 'tensor')
- fresh_down_second_moment: float32 [16, 8192, 64], P('dp', 'tensor')
- fresh_adapter_up: float32 [16, 64, 8192], P('dp', None, 'tensor')
- fresh_up_first_moment: float32 [16, 64, 8192], P('dp', None, 'tensor')
- fresh_up_second_moment: float32 [16, 64, 8192], P('dp', None, 'tensor')
The draws below stay inside these ranges and needn't reach their ends.
Inputs may be any that keep to these rules, and one draw needn't show every extreme that they name: `tenant_lookup`: tenants own contiguous runs of dp indices, numbered in order; every tenant owns at least one index and the largest owns 16 - 3. `active_token_rows`: multiples of 128; some dp index has all 384 slots live.
All inputs are finite; a program needn't handle non-finite values.
Results may differ from the reference program's by a relative error of at most 0.0037.
Values may be sent and summed in bfloat16 or wider, within the bound.
A program may use at most 256 MiB of HBM per device.

```python
import math
import jax
import jax.numpy as jnp
import numpy as np
from jax import lax

MODEL_WIDTH = 8192
ADAPTER_RANK = 64
TENANTS = 4
ADAM_STEP = 10
TOK_DP = 384
TOKENS = 6144
N_DP = 16


def draw_active_token_rows(key, part):
    key = jax.random.fold_in(key, 7)
    first_key, second_key = jax.random.split(key)
    blocks = jax.random.randint(first_key, (N_DP,), 1, TOK_DP // 128 + 1)
    fullest = jax.random.randint(second_key, (), 0, N_DP)
    blocks = jnp.where(jnp.arange(N_DP) == fullest, TOK_DP // 128, blocks)
    return (blocks * 128).astype(jnp.int32)


def shared_rows(key):
    common_key, noise_key = jax.random.split(key)
    common = jax.random.normal(common_key, (1, MODEL_WIDTH), jnp.float32)
    noise = jax.random.normal(noise_key, (TOKENS, MODEL_WIDTH), jnp.float32)
    return jnp.clip(common + noise, -6.0, 6.0).astype(jnp.bfloat16)


def draw_output_gradient(key, part):
    key = jax.random.fold_in(key, 11)
    return shared_rows(key)


def draw_attention_input(key, part):
    key = jax.random.fold_in(key, 13)
    return shared_rows(key)


def steps_of(key, shape, shards, smallest, top_value):
    def one(dim, blocks):
        draws = jax.random.uniform(jax.random.fold_in(jax.random.fold_in(key, 6), dim), (blocks,), jnp.float32, smallest / len(shards), top_value / len(shards))
        return jnp.repeat(jnp.exp(draws), shape[dim] // blocks).reshape((-1,) + (1,) * (len(shape) - dim - 1))

    loudness = one(*shards[0])
    for cut in shards[1:]:
        loudness = loudness * one(*cut)
    return loudness


def length_profile(count, total, reach, lean):
    loads = [(1 << 20) // math.isqrt(grade ** lean) + 1 for grade in range(2, count + 1)]
    spare, counts = total - reach - (count - 1), [1] * (count - 1)
    while spare > 0:
        free = [i for i in range(count - 1) if counts[i] < reach]
        pool, remaining = sum([loads[i] for i in free]), spare
        for i in free:
            extra = min(reach - counts[i], max(1, remaining * loads[i] // pool), spare)
            counts[i] = counts[i] + extra
            spare = spare - extra
    return np.array([reach] + counts)


def ragged(rng, count, total, reach, lean):
    if count == 2:
        one = jax.random.randint(rng, (), max(1, total - reach), min(reach, total - 1) + 1)
        return jnp.stack([one, total - one])
    lengths = jnp.asarray(length_profile(count, total, reach, lean), jnp.int32)
    twos = (count - 1) // 2
    donor, sink = lengths[1:1 + 2 * twos:2], lengths[2:2 + 2 * twos:2]
    slack = jnp.minimum(donor - 1, reach - sink)
    moved = jax.random.randint(jax.random.fold_in(rng, 1), (twos,), 0, 1 << 20) % (slack + 1)
    lengths = lengths.at[1:1 + 2 * twos:2].set(donor - moved).at[2:2 + 2 * twos:2].set(sink + moved)
    return lengths[jax.random.permutation(jax.random.fold_in(rng, 2), count)]


def normal_values(rng, dims, scale, bound, cuts=(), kind=jnp.bfloat16):
    result = scale * jax.random.normal(rng, dims, jnp.float32)
    if cuts:
        result = result * steps_of(rng, dims, cuts, -0.22, 0.18)
    return jnp.clip(result, -bound, bound).astype(kind)


def setup_inputs(seed: int = 0) -> dict:
    seeds = jax.random.split(jax.random.key(seed), 12)
    output_gradient = draw_output_gradient(jax.random.fold_in(seeds[11], 71), 0)
    attention_input = draw_attention_input(jax.random.fold_in(seeds[11], 71), 0)
    projection_weight = normal_values(seeds[2], (MODEL_WIDTH, MODEL_WIDTH), MODEL_WIDTH ** -0.5, 0.0625, ((0, 2), (1, 16)))
    adapter_down = normal_values(seeds[3], (N_DP, MODEL_WIDTH, ADAPTER_RANK), MODEL_WIDTH ** -0.5, 0.0625, ((0, 16), (1, 2)), jnp.float32)
    adapter_up = normal_values(seeds[4], (N_DP, ADAPTER_RANK, MODEL_WIDTH), MODEL_WIDTH ** -0.5, 0.0625, ((0, 16), (2, 2)), jnp.float32)
    down_first_moment = normal_values(seeds[5], (N_DP, MODEL_WIDTH, ADAPTER_RANK), 0.05, 0.75, ((0, 16), (1, 2)), jnp.float32)
    down_second_moment = jnp.clip(jnp.exp(math.log(0.01) - 2.30258502 * jax.random.uniform(seeds[6], (N_DP, MODEL_WIDTH, ADAPTER_RANK), jnp.float32) ** steps_of(seeds[6], (N_DP, MODEL_WIDTH, ADAPTER_RANK), ((0, 16), (1, 2)), -0.2, 0.2)), 0.001, 0.01)
    up_first_moment = normal_values(seeds[7], (N_DP, ADAPTER_RANK, MODEL_WIDTH), 0.05, 0.75, ((0, 16), (2, 2)), jnp.float32)
    up_second_moment = jnp.clip(jnp.exp(math.log(0.01) - 2.30258502 * jax.random.uniform(seeds[8], (N_DP, ADAPTER_RANK, MODEL_WIDTH), jnp.float32) ** steps_of(seeds[8], (N_DP, ADAPTER_RANK, MODEL_WIDTH), ((0, 16), (2, 2)), -0.2, 0.2)), 0.001, 0.01)
    tenant_lookup = jnp.searchsorted(jnp.cumsum(ragged(seeds[9], TENANTS, N_DP, N_DP - TENANTS + 1, 2)), jnp.arange(N_DP), side="right").astype(jnp.int32)
    active_token_rows = draw_active_token_rows(jax.random.fold_in(seeds[11], 71), 0)
    return dict(output_gradient=output_gradient, attention_input=attention_input, projection_weight=projection_weight, adapter_down=adapter_down, adapter_up=adapter_up, down_first_moment=down_first_moment, down_second_moment=down_second_moment, up_first_moment=up_first_moment, up_second_moment=up_second_moment, tenant_lookup=tenant_lookup, active_token_rows=active_token_rows)


adapter_scale = 2.0
beta_one = 0.9
beta_two = 0.999
learn_rate = 0.02
adam_eps = 1e-08

def apply_adam_rule(param, grad, moment, second):
    new_moment = beta_one * moment + (1.0 - beta_one) * grad
    new_second = beta_two * second + (1.0 - beta_two) * grad * grad
    fix_one = 1.0 - beta_one ** ADAM_STEP
    fix_two = 1.0 - beta_two ** ADAM_STEP
    step_size = new_moment / fix_one / (jnp.sqrt(new_second / fix_two) + adam_eps)
    return (param - learn_rate * step_size, new_moment, new_second)

def reference(output_gradient, attention_input, projection_weight, adapter_down, adapter_up, down_first_moment, down_second_moment, up_first_moment, up_second_moment, tenant_lookup, active_token_rows):
    grand_total = output_gradient.shape[0]
    feature_width = output_gradient.shape[1]
    slot = jnp.arange(grand_total, dtype=jnp.int32)
    owner = slot // TOK_DP
    keep = slot % TOK_DP < active_token_rows[owner]
    masked = jnp.where(keep[:, None], output_gradient, jnp.zeros_like(output_gradient))
    down_portion = adapter_down.astype(jnp.bfloat16)
    up_portion = adapter_up.astype(jnp.bfloat16)
    output_gradient_blocks = masked.reshape(N_DP, TOK_DP, feature_width).astype(jnp.float32)
    input_blocks = attention_input.reshape(N_DP, TOK_DP, feature_width).astype(jnp.float32)
    rank_space_input = jnp.einsum('ntd,ndr->ntr', input_blocks, down_portion.astype(jnp.float32)).astype(jnp.bfloat16)
    rank_space_gradient = jnp.einsum('ntd,nrd->ntr', output_gradient_blocks, up_portion.astype(jnp.float32)).astype(jnp.bfloat16)
    frozen_gradient = jnp.dot(masked, projection_weight.T, preferred_element_type=jnp.float32)
    adapter_contribution = jnp.einsum('cem,czm->cez', rank_space_gradient.astype(jnp.float32), down_portion.astype(jnp.float32))
    input_gradient = (frozen_gradient + adapter_scale * adapter_contribution.reshape(grand_total, feature_width)).astype(jnp.bfloat16)
    down_partial = adapter_scale * jnp.einsum('iyu,iyh->iuh', input_blocks, rank_space_gradient.astype(jnp.float32))
    up_partial = adapter_scale * jnp.einsum('jxl,jxw->jlw', rank_space_input.astype(jnp.float32), output_gradient_blocks)
    onehot = (tenant_lookup[:, None] == jnp.arange(TENANTS, dtype=jnp.int32)[None, :]).astype(jnp.float32)
    sum_a = jnp.einsum('nk,ndr->kdr', onehot, down_partial, precision=lax.Precision.HIGHEST)
    sum_b = jnp.einsum('nk,nrd->krd', onehot, up_partial, precision=lax.Precision.HIGHEST)
    count = jnp.einsum('nk,n->k', onehot, active_token_rows.astype(jnp.float32), precision=lax.Precision.HIGHEST)
    down_gradient = sum_a[tenant_lookup] / count[tenant_lookup][:, None, None]
    up_gradient = sum_b[tenant_lookup] / count[tenant_lookup][:, None, None]
    fresh_adapter_down, fresh_down_first_moment, fresh_down_second_moment = apply_adam_rule(adapter_down, down_gradient, down_first_moment, down_second_moment)
    fresh_adapter_up, fresh_up_first_moment, fresh_up_second_moment = apply_adam_rule(adapter_up, up_gradient, up_first_moment, up_second_moment)
    return (input_gradient, fresh_adapter_down, fresh_down_first_moment, fresh_down_second_moment, fresh_adapter_up, fresh_up_first_moment, fresh_up_second_moment)
```

```python
import jax
import jax.numpy as jnp
from jax import lax
from jax.experimental import pallas as pl
from jax.experimental.pallas import tpu as pltpu
from jax.sharding import PartitionSpec as P

TENANTS = 4
ADAM_STEP = 10


adapter_scale = 2.0
beta_one = 0.9
beta_two = 0.999
learn_rate = 0.02
adam_eps = 1e-08


def apply_adam_rule(param, grad, moment, second):
    new_moment = beta_one * moment + (1.0 - beta_one) * grad
    new_second = beta_two * second + (1.0 - beta_two) * grad * grad
    fix_one = 1.0 - beta_one**ADAM_STEP
    fix_two = 1.0 - beta_two**ADAM_STEP
    step_size = new_moment / fix_one / (jnp.sqrt(new_second / fix_two) + adam_eps)
    return (param - learn_rate * step_size, new_moment, new_second)


def contract_trailing(left, right):
    return lax.dot_general(
        left, right, (((1,), (1,)), ((), ())), preferred_element_type=jnp.float32
    )


def contract_leading(left, right):
    return lax.dot_general(
        left, right, (((0,), (0,)), ((), ())), preferred_element_type=jnp.float32
    )


def on_device(
    output_gradient,
    attention_input,
    projection_weight,
    adapter_down,
    adapter_up,
    down_first_moment,
    down_second_moment,
    up_first_moment,
    up_second_moment,
    tenant_lookup,
    active_token_rows,
):
    tensor_pos = lax.axis_index("tensor")
    dp_pos = lax.axis_index("dp")
    shard_rows = output_gradient.shape[0]
    columns = attention_input.shape[1]
    positions = tensor_pos * shard_rows + jnp.arange(shard_rows, dtype=jnp.int32)
    masked = jnp.where(
        (positions < active_token_rows[0])[:, None],
        output_gradient,
        jnp.zeros_like(output_gradient),
    )
    down_portion = adapter_down[0].astype(jnp.bfloat16)
    up_portion = adapter_up[0].astype(jnp.bfloat16)
    gathered = lax.all_gather(masked, "tensor", axis=0, tiled=True)
    frozen_gradient = contract_trailing(
        gathered, lax.all_gather(projection_weight, "dp", axis=1, tiled=True)
    )
    tenant_match_mask = lax.dynamic_slice_in_dim(gathered, tensor_pos * columns, columns, 1)
    in_part = jnp.dot(attention_input, down_portion, preferred_element_type=jnp.float32)
    grad_part = contract_trailing(tenant_match_mask, up_portion)
    rank_space_input, rank_space_gradient = lax.psum((in_part, grad_part), "tensor")
    rank_space_input = rank_space_input.astype(jnp.bfloat16)
    rank_space_gradient = rank_space_gradient.astype(jnp.bfloat16)
    input_gradient = (
        frozen_gradient + adapter_scale * contract_trailing(rank_space_gradient, down_portion)
    ).astype(jnp.bfloat16)
    down_partial = adapter_scale * contract_leading(attention_input, rank_space_gradient)
    up_partial = adapter_scale * contract_leading(rank_space_input, tenant_match_mask)
    live_count = active_token_rows[0].astype(jnp.float32)
    own_tenant = tenant_lookup[dp_pos]
    slots = (jnp.arange(TENANTS, dtype=jnp.int32) == own_tenant).astype(jnp.float32)
    slot_a = slots[:, None, None] * down_partial[None]
    slot_b = slots[:, None, None] * up_partial[None]
    slot_count = slots * live_count
    total_a, total_b, total_count = lax.psum((slot_a, slot_b, slot_count), "dp")
    sum_a = lax.dynamic_index_in_dim(total_a, own_tenant, 0, keepdims=False)
    sum_b = lax.dynamic_index_in_dim(total_b, own_tenant, 0, keepdims=False)
    count = lax.dynamic_index_in_dim(total_count, own_tenant, 0, keepdims=False)
    down_gradient = sum_a / count
    up_gradient = sum_b / count
    fresh_adapter_down, fresh_down_first_moment, fresh_down_second_moment = apply_adam_rule(
        adapter_down[0], down_gradient, down_first_moment[0], down_second_moment[0]
    )
    fresh_adapter_up, fresh_up_first_moment, fresh_up_second_moment = apply_adam_rule(
        adapter_up[0], up_gradient, up_first_moment[0], up_second_moment[0]
    )
    return (
        input_gradient,
        fresh_adapter_down[None],
        fresh_down_first_moment[None],
        fresh_down_second_moment[None],
        fresh_adapter_up[None],
        fresh_up_first_moment[None],
        fresh_up_second_moment[None],
    )


MESH = pl.DeviceIdType.MESH
CHUNKS = 16
LOW_STEP = 6
OUT_STEP = 7
EXTRA = 8


def fused_kernel(
    g, attn, w, a_half, b_half, lookup, live,
    out, sums,
    wbuf, gk, gx, attn_v, precv, psend, acc, low_out, low_in_buf, lin, lgr, part, lay,
    up_in, down_in, up_out, down_out,
    local_sem, w_send, w_recv, g_send, g_recv, p_send, p_recv, o_sem, lr_sem,
    part_send, part_recv, chain_send, chain_recv, fin_send, fin_recv,
):
    dp = lax.axis_index("dp")
    x = lax.axis_index("tensor")
    z, y, c = dp // 4, (dp // 2) % 2, dp % 2
    me = dp % 4
    rows, width = g.shape
    both = 2 * rows
    columns, kblk = w.shape
    cn = columns // CHUNKS
    span = 2 * kblk
    half = width // 2
    piece = columns // 4
    rank = b_half.shape[0]

    here = {"dp": dp, "tensor": x}
    across = {"dp": dp, "tensor": 1 - x}
    y_dp = z * 4 + (1 - y) * 2 + c
    y_peer = {"dp": y_dp, "tensor": x}
    diag = {"dp": y_dp, "tensor": 1 - x}
    sibling = {"dp": dp - c + (1 - c), "tensor": x}
    corner = {"dp": z * 4 + (1 - y) * 2 + (1 - c), "tensor": x}
    above = {"dp": lax.rem(dp + 4, 16), "tensor": x}
    below = {"dp": lax.rem(dp + 12, 16), "tensor": x}

    barrier = pltpu.get_barrier_semaphore()
    for other in (across, y_peer, diag, sibling, corner):
        pl.semaphore_signal(barrier, inc=1, device_id=other, device_id_type=MESH)

    @pl.when(z < 3)
    def _():
        pl.semaphore_signal(barrier, inc=1, device_id=above, device_id_type=MESH)

    @pl.when(z > 0)
    def _():
        pl.semaphore_signal(barrier, inc=1, device_id=below, device_id_type=MESH)

    pl.semaphore_wait(barrier, 5 + (z < 3).astype(jnp.int32) + (z > 0).astype(jnp.int32))

    def remote(src, dst, send, recv, where):
        return pltpu.make_async_remote_copy(
            src_ref=src, dst_ref=dst, send_sem=send, recv_sem=recv,
            device_id=where, device_id_type=MESH,
        )

    def w_slot(layer, core, n):
        return wbuf.at[
            pl.ds(pl.multiple_of(n * cn, cn), cn),
            pl.ds(pl.multiple_of(layer * span + core * kblk, kblk), kblk),
        ]

    def w_copy(layer, n, way):
        slot = w_slot(layer, c, n)
        where = (above, below, sibling)[way]
        return remote(
            slot, slot, w_send.at[layer, way, n], w_recv.at[layer, way // 2, n], where
        )

    def own_copy(n, way):
        where = (above, below, sibling)[way]
        return remote(
            w.at[pl.ds(pl.multiple_of(n * cn, cn), cn), :], w_slot(z, c, n),
            w_send.at[z, way, n], w_recv.at[z, way // 2, n], where,
        )

    def own_start(n):
        @pl.when(z < 3)
        def _():
            own_copy(n, 0).start()

        @pl.when(z > 0)
        def _():
            own_copy(n, 1).start()

        own_copy(n, 2).start()

    def w_wait(layer, core, way, n):
        slot = w_slot(layer, core, n)
        remote(slot, slot, w_send.at[layer, 2, n], w_recv.at[layer, way, n], sibling).wait_recv()

    def relay(dist, n):
        @pl.when(z >= dist)
        def _():
            w_wait(z - dist, c, 0, n)

            @pl.when(z < 3)
            def _():
                w_copy(z - dist, n, 0).start()

            w_copy(z - dist, n, 2).start()

        @pl.when(z + dist <= 3)
        def _():
            w_wait(z + dist, c, 0, n)

            @pl.when(z > 0)
            def _():
                w_copy(z + dist, n, 1).start()

            w_copy(z + dist, n, 2).start()

    mine = pl.ds(pl.multiple_of(x * rows, rows), rows)
    theirs = pl.ds(pl.multiple_of(both + x * rows, rows), rows)

    def g_cols(layer, line):
        return g.at[:, pl.ds(pl.multiple_of(layer * 2 * span + line * span, span), span)]

    def g_copies():
        copies = [
            remote(
                g.at[:, pl.ds(pl.multiple_of((1 - x) * half, half), half)],
                gx.at[mine, :], g_send.at[12], g_recv.at[12], across,
            )
        ]
        for k in range(4):
            cols = pl.ds(k * span, span)
            copies.append(remote(g_cols(k, y), gk.at[mine, cols], g_send.at[k], g_recv.at[k], across))
            copies.append(remote(g_cols(k, 1 - y), gk.at[theirs, cols], g_send.at[4 + k], g_recv.at[4 + k], y_peer))
            copies.append(remote(g_cols(k, 1 - y), gk.at[theirs, cols], g_send.at[8 + k], g_recv.at[8 + k], diag))
        return copies

    def g_arrivals():
        row_x = pl.ds(pl.multiple_of((1 - x) * rows, rows), rows)
        row_y = pl.ds(pl.multiple_of(both + x * rows, rows), rows)
        row_d = pl.ds(pl.multiple_of(both + (1 - x) * rows, rows), rows)
        remote(gx.at[row_x, :], gx.at[row_x, :], g_send.at[12], g_recv.at[12], across).wait_recv()
        for k in range(4):
            cols = pl.ds(k * span, span)
            for base, where in ((0, row_x), (4, row_y), (8, row_d)):
                spot = gk.at[where, cols]
                remote(spot, spot, g_send.at[base + k], g_recv.at[base + k], across).wait_recv()

    def local_copies():
        copies = [
            pltpu.make_async_copy(attn, attn_v, local_sem.at[0]),
            pltpu.make_async_copy(
                w, wbuf.at[:, pl.ds(pl.multiple_of(z * span + c * kblk, kblk), kblk)], local_sem.at[1]
            ),
            pltpu.make_async_copy(
                g.at[:, pl.ds(pl.multiple_of(x * half, half), half)], gx.at[mine, :], local_sem.at[2]
            ),
        ]
        for k in range(4):
            copies.append(pltpu.make_async_copy(
                g_cols(k, y), gk.at[mine, pl.ds(k * span, span)], local_sem.at[3 + k]
            ))
        return copies

    own_start(0)
    for copy in g_copies():
        copy.start()
    for copy in local_copies():
        copy.start()

    keep = lax.broadcasted_iota(jnp.int32, (both, 1), 0) < live[0]

    def low_copy():
        return remote(low_out, low_in_buf, lr_sem.at[0], lr_sem.at[1], across)

    def low_first():
        for copy in local_copies():
            copy.wait()
        g_arrivals()
        low_out[:, :rank] = jnp.dot(attn_v[...], a_half[...], preferred_element_type=jnp.float32)
        low_out[:, rank:] = contract_trailing(gx[...], b_half[...])
        low_copy().start()

    mates = [
        {"dp": z * 4 + q, "tensor": x} for q in range(4)
    ]

    def part_copy(q):
        return remote(part.at[q], lay.at[me], part_send.at[q], part_recv.at[me], mates[q])

    def low_second():
        low_copy().wait()
        total = low_out[...] + low_in_buf[...]
        low_in = total[:, :rank].astype(jnp.bfloat16)
        low_grad = total[:, rank:].astype(jnp.bfloat16)
        zero = jnp.zeros_like(low_in)
        lin[...] = jnp.where(keep, low_in, zero)
        lgr[...] = jnp.where(keep, low_grad, zero)
        for q in range(4):
            cols = pl.ds(q * piece, piece)
            part[q, :rank, :] = adapter_scale * contract_leading(lgr[...], attn_v[:, cols])
            part[q, rank : 2 * rank, :] = adapter_scale * contract_leading(lin[...], gx[:, cols])
            part[q, 2 * rank :, :] = jnp.full((EXTRA, piece), live[0].astype(jnp.float32))
            copy = part_copy(q)

            @pl.when(q != me)
            def _(copy=copy):
                copy.start()

    def parts_in():
        for q in range(4):
            @pl.when(q != me)
            def _(q=q):
                remote(lay.at[q], lay.at[q], part_send.at[q], part_recv.at[q], sibling).wait_recv()

            @pl.when(q == me)
            def _(q=q):
                lay[q] = part[q]

    tall = 2 * rank + EXTRA

    def tenant(i):
        return lookup[i]

    def sum_of(who, where):
        total = None
        for q in range(4):
            term = jnp.where(tenant(z * 4 + q) == who, lay[q, where, :], 0.0)
            total = term if total is None else total + term
        return total

    low_nb = jnp.maximum(z * 4 - 1, 0)
    high_nb = jnp.minimum(z * 4 + 4, 15)

    def chain_copy(way):
        if way == 0:
            return remote(up_out, up_in, chain_send.at[0], chain_recv.at[0], above)
        return remote(down_out, down_in, chain_send.at[1], chain_recv.at[1], below)

    def go_up():
        who = tenant(z * 4 + 3)

        @pl.when(z > 0)
        def _():
            remote(up_in, up_in, chain_send.at[0], chain_recv.at[0], below).wait_recv()

        @pl.when(z == 0)
        def _():
            up_in[...] = jnp.zeros_like(up_in)

        def body(i, _):
            where = pl.ds(pl.multiple_of(i * 8, 8), 8)
            joined = jnp.where(tenant(low_nb) == who, up_in[where, :], 0.0)
            up_out[where, :] = sum_of(who, where) + joined
            return 0

        lax.fori_loop(0, tall // 8, body, 0)

        @pl.when(z < 3)
        def _():
            chain_copy(0).start()

    def go_down():
        who = tenant(z * 4)

        @pl.when(z < 3)
        def _():
            remote(down_in, down_in, chain_send.at[1], chain_recv.at[1], above).wait_recv()

        @pl.when(z == 3)
        def _():
            down_in[...] = jnp.zeros_like(down_in)

        def body(i, _):
            where = pl.ds(pl.multiple_of(i * 8, 8), 8)
            joined = jnp.where(tenant(high_nb) == who, down_in[where, :], 0.0)
            down_out[where, :] = sum_of(who, where) + joined
            return 0

        lax.fori_loop(0, tall // 8, body, 0)

        @pl.when(z > 0)
        def _():
            chain_copy(1).start()

    def fin_copy(q):
        return remote(lay.at[q], sums.at[me], fin_send.at[q], fin_recv.at[me], mates[q])

    def own_sum(q):
        return pltpu.make_async_copy(lay.at[q], sums.at[q], local_sem.at[7])

    def totals():
        def body(i, _):
            where = pl.ds(pl.multiple_of(i * 8, 8), 8)
            old = [lay[q, where, :] for q in range(4)]
            lower, upper = up_in[where, :], down_in[where, :]
            for q in range(4):
                who = tenant(z * 4 + q)
                total = jnp.where(tenant(low_nb) == who, lower, 0.0)
                total = total + jnp.where(tenant(high_nb) == who, upper, 0.0)
                for k in range(4):
                    total = total + jnp.where(tenant(z * 4 + k) == who, old[k], 0.0)
                lay[q, where, :] = total
            return 0

        lax.fori_loop(0, tall // 8, body, 0)
        for q in range(4):
            @pl.when(q != me)
            def _(q=q):
                fin_copy(q).start()

            @pl.when(q == me)
            def _(q=q):
                own_sum(q).start()

    slots = psend.shape[0]

    def p_copy(n):
        return remote(
            psend.at[n % slots], precv.at[n], p_send.at[n], p_recv.at[n], y_peer
        )

    def product(n, _):
        for k in range(4):
            w_wait(k, 1 - c, 1, n)

        @pl.when(n >= slots)
        def _():
            p_copy(n - slots).wait_send()

        block = wbuf[pl.ds(pl.multiple_of(n * cn, cn), cn), :]
        acc[n % slots] = contract_trailing(gk[:both, :], block)
        psend[n % slots] = contract_trailing(gk[both:, :], block).astype(jnp.bfloat16)
        p_copy(n).start()
        return 0

    def o_copy(n):
        return pltpu.make_async_copy(
            precv.at[n], out.at[:, pl.ds(pl.multiple_of(n * cn, cn), cn)], o_sem.at[n]
        )

    def finish(n, _):
        remote(precv.at[n], precv.at[n], p_send.at[n], p_recv.at[n], y_peer).wait_recv()
        low = contract_trailing(lgr[...], a_half[pl.ds(pl.multiple_of(n * cn, cn), cn), :])
        total = acc[n % slots] + precv[n].astype(jnp.float32) + adapter_scale * low
        precv[n] = jnp.where(keep, total, 0.0).astype(jnp.bfloat16)
        o_copy(n).start()
        return 0

    def done(s):
        goal = jnp.minimum(2 * (s - OUT_STEP + 1), s - 2)
        return jnp.clip(goal, 0, CHUNKS)

    def step(s, _):
        @pl.when(s + 1 < CHUNKS)
        def _():
            own_start(s + 1)

        for dist in (1, 2, 3):
            n = s - (dist - 1)

            @pl.when((n >= 0) & (n < CHUNKS))
            def _(dist=dist, n=n):
                relay(dist, n)

        @pl.when(s == LOW_STEP)
        def _():
            low_first()

        @pl.when(s == LOW_STEP + 1)
        def _():
            low_second()

        @pl.when(s == LOW_STEP + 2)
        def _():
            parts_in()

        @pl.when(s == LOW_STEP + 2 + z)
        def _():
            go_up()

        @pl.when(s == LOW_STEP + 5 - z)
        def _():
            go_down()

        @pl.when(s == LOW_STEP + 6)
        def _():
            totals()

        lax.fori_loop(done(s - 1), done(s), product, 0)
        lax.fori_loop(done(s - 2), done(s - 1), finish, 0)
        return 0

    lax.fori_loop(0, CHUNKS + 4, step, 0)

    for copy in g_copies():
        copy.wait_send()
    for q in range(4):
        @pl.when(q != me)
        def _(q=q):
            part_copy(q).wait_send()
            fin_copy(q).wait_send()
            remote(lay.at[q], sums.at[q], fin_send.at[q], fin_recv.at[q], sibling).wait_recv()

        @pl.when(q == me)
        def _(q=q):
            own_sum(q).wait()

    @pl.when(z < 3)
    def _():
        chain_copy(0).wait_send()

    @pl.when(z > 0)
    def _():
        chain_copy(1).wait_send()

    def drain(n, _):
        o_copy(n).wait()

        @pl.when(n >= CHUNKS - slots)
        def _():
            p_copy(n).wait_send()

        for k in range(4):
            w_copy(k, n, 2).wait_send()

            @pl.when((z < 3) & (k <= z))
            def _(k=k):
                w_copy(k, n, 0).wait_send()

            @pl.when((z > 0) & (k >= z))
            def _(k=k):
                w_copy(k, n, 1).wait_send()

        return 0

    lax.fori_loop(0, CHUNKS, drain, 0)


def on_device_fused(
    output_gradient,
    attention_input,
    projection_weight,
    adapter_down,
    adapter_up,
    down_first_moment,
    down_second_moment,
    up_first_moment,
    up_second_moment,
    tenant_lookup,
    active_token_rows,
):
    rows, width = output_gradient.shape
    both, columns = attention_input.shape
    rank = adapter_up.shape[1]
    cn = columns // CHUNKS
    piece = columns // 4
    tall = 2 * rank + EXTRA
    bf16, f32 = jnp.bfloat16, jnp.float32
    dma = pltpu.SemaphoreType.DMA
    hbm = pl.BlockSpec(memory_space=pl.ANY)
    vmem = pl.BlockSpec(memory_space=pltpu.VMEM)
    smem = pl.BlockSpec(memory_space=pltpu.SMEM)
    input_gradient, sums = pl.pallas_call(
        fused_kernel,
        out_shape=(
            jax.ShapeDtypeStruct((both, columns), bf16),
            jax.ShapeDtypeStruct((4, tall, piece), f32),
        ),
        in_specs=[hbm, hbm, hbm, vmem, vmem, smem, smem],
        out_specs=(hbm, hbm),
        scratch_shapes=[
            pltpu.VMEM((columns, width // 2), bf16),
            pltpu.VMEM((2 * both, width // 2), bf16),
            pltpu.VMEM((both, width // 2), bf16),
            pltpu.VMEM((both, columns), bf16),
            pltpu.VMEM((CHUNKS, both, cn), bf16),
            pltpu.VMEM((4, both, cn), bf16),
            pltpu.VMEM((4, both, cn), f32),
            pltpu.VMEM((both, 2 * rank), f32),
            pltpu.VMEM((both, 2 * rank), f32),
            pltpu.VMEM((both, rank), bf16),
            pltpu.VMEM((both, rank), bf16),
            pltpu.VMEM((4, tall, piece), f32),
            pltpu.VMEM((4, tall, piece), f32),
            pltpu.VMEM((tall, piece), f32),
            pltpu.VMEM((tall, piece), f32),
            pltpu.VMEM((tall, piece), f32),
            pltpu.VMEM((tall, piece), f32),
            dma((8,)),
            dma((4, 3, CHUNKS)),
            dma((4, 2, CHUNKS)),
            dma((13,)),
            dma((13,)),
            dma((CHUNKS,)),
            dma((CHUNKS,)),
            dma((CHUNKS,)),
            dma((2,)),
            dma((4,)),
            dma((4,)),
            dma((2,)),
            dma((2,)),
            dma((4,)),
            dma((4,)),
        ],
        compiler_params=pltpu.CompilerParams(
            collective_id=0, has_side_effects=True, vmem_limit_bytes=63 * 1024 * 1024
        ),
        cost_estimate=pl.CostEstimate(
            flops=2 * both * columns * width, bytes_accessed=64 * 1024 * 1024, transcendentals=0
        ),
    )(
        output_gradient,
        attention_input,
        projection_weight,
        adapter_down[0].astype(bf16),
        adapter_up[0].astype(bf16),
        tenant_lookup,
        active_token_rows,
    )
    count = sums[0, 2 * rank, 0]
    down_gradient = sums[:, :rank, :].transpose(0, 2, 1).reshape(columns, rank) / count
    up_gradient = sums[:, rank : 2 * rank, :].transpose(1, 0, 2).reshape(rank, columns) / count
    fresh_down = apply_adam_rule(
        adapter_down[0], down_gradient, down_first_moment[0], down_second_moment[0]
    )
    fresh_up = apply_adam_rule(adapter_up[0], up_gradient, up_first_moment[0], up_second_moment[0])
    return (input_gradient,) + tuple(v[None] for v in fresh_down + fresh_up)


def solution(mesh):
    fused = mesh.shape["tensor"] == 2 and mesh.shape["dp"] == 16
    return jax.shard_map(
        on_device_fused if fused else on_device,
        mesh=mesh,
        in_specs=(
            P(("dp", "tensor"), None),
            P("dp", "tensor"),
            P("tensor", "dp"),
            P("dp", "tensor", None),
            P("dp", None, "tensor"),
            P("dp", "tensor", None),
            P("dp", "tensor", None),
            P("dp", None, "tensor"),
            P("dp", None, "tensor"),
            P(),
            P("dp"),
        ),
        out_specs=(
            P("dp", "tensor"),
            P("dp", "tensor", None),
            P("dp", "tensor", None),
            P("dp", "tensor", None),
            P("dp", None, "tensor"),
            P("dp", None, "tensor"),
            P("dp", None, "tensor"),
        ),
        check_vma=False,
    )
```
